32 devices in a mesh: grp: 2 (over y), gx: 4 (over z), gy: 4 (over x, core).
Axes of the slice: x: 2, y: 2, z: 4, core: 2. Of those that a mesh axis runs over, the one named last changes fastest.
Arguments:
- stream_in: bfloat16 [128, 8192], P(('grp', 'gy'), 'gx'), parts along dimension 0, may hold values from -0.59765625 to 0.59765625
- attention_gain: float32 [8192], P('gx'), may hold values from 0.1 to 1.9
- dense_gain: float32 [8192], P('gx'), may hold values from 0.1 to 1.9
- w_query: bfloat16 [8192, 8192], P('gx', 'gy'), may hold values from -0.0625 to 0.0625
- w_keyval: bfloat16 [8192, 1024], P('gx'), may hold values from -0.0625 to 0.0625
- w_out: bfloat16 [8192, 8192], P('gy', 'gx'), may hold values from -0.0625 to 0.0625
- gate_up: bfloat16 [8192, 2, 26624], P('gx', None, 'gy'), may hold values from -0.0625 to 0.0625
- cache_entries: bfloat16 [128, 2, 384, 512], P(('grp', 'gx', 'gy')), parts along dimension 0, as said below
- lengths: int32 [128], P(('grp', 'gx', 'gy')), parts along dimension 0, may hold values from 1 to 384, as said below
Outputs:
- stream: bfloat16 [128, 8192], P(('grp', 'gy'), 'gx'), parts along dimension 0
- mlp_hidden: bfloat16 [128, 26624], P(('grp', 'gx'), 'gy'), parts along dimension 0
- new_entries: bfloat16 [128, 1024], P(('grp', 'gx', 'gy')), parts along dimension 0
The draws below stay inside these ranges and needn't reach their ends.
There are 2 independent parts, one for each index of `grp`. The reference program is written for one: setup_inputs(seed, part) draws one part's arguments, and reference() takes and returns one part's arrays. A program takes and returns all parts, laid end to end along the dimension named above; an argument that names none is the same for every part. Nothing has to cross between parts.
Inputs may be any that keep to these rules, and one draw needn't show every extreme that they name: `lengths`: cache slots at or past a row's length are never read; some row in every draw has exactly 384. `cache_entries`: keys are stored already rotated.
All inputs are finite; a program needn't handle non-finite values.
Results may differ from the reference program's by a relative error of at most 0.025.
The reference program's roundings to bfloat16 on the way count: a program that leaves them out, or rounds other values in their place, can miss the bound.
Values may be sent and summed in bfloat16 or wider, within the bound.
No kernel may reach another device: no remote copies, remote signals or barrier semaphores. Data moves between devices by JAX's collectives and lax.ppermute only.
A program may use at most 256 MiB of HBM per device.

```python
import math
import jax
import jax.numpy as jnp
from jax import lax

D = 8192
HD = 128
QH = 64
KVH = 4
FF = 26624
CACHE = 384
ROWS_DEV = 4
QW = 8192
KVW = 512
ROWS = 64
N_GX = 4


def draw_lengths(key, part):
    key = jax.random.fold_in(key, 11)
    first_key, second_key, pick_key = jax.random.split(key, 3)
    front = jax.random.randint(first_key, (ROWS,), 0, CACHE, dtype=jnp.int32)
    back = jax.random.randint(second_key, (ROWS,), 0, CACHE, dtype=jnp.int32)
    drawn = 1 + front * back // CACHE
    chosen = jax.random.randint(pick_key, (), 0, ROWS, dtype=jnp.int32)
    return jnp.where(jnp.arange(ROWS, dtype=jnp.int32) == chosen, CACHE, drawn).astype(jnp.int32)


def draw_cache_entries(key, part):
    key = jax.random.fold_in(key, 23)
    base_key = jax.random.fold_in(key, 0)
    values = jax.random.normal(base_key, (ROWS, 2, CACHE, KVW), jnp.float32)
    return values.astype(jnp.bfloat16)


def level_of(own_key, shape, pieces, low, largest):
    def one(position, parts):
        draws = jax.random.uniform(jax.random.fold_in(jax.random.fold_in(own_key, 6), position), (parts,), jnp.float32, low / len(pieces), largest / len(pieces))
        return jnp.repeat(jnp.exp(draws), shape[position] // parts).reshape((-1,) + (1,) * (len(shape) - position - 1))

    factor_of = one(*pieces[0])
    for cut in pieces[1:]:
        factor_of = factor_of * one(*cut)
    return factor_of


def bell_draw(own_key, dims, scale, bound, cuts=(), kind=jnp.bfloat16):
    loudness = level_of(own_key, dims, cuts, -0.22, 0.18) if cuts else 1.0
    values = jax.random.normal(own_key, dims, jnp.float32) * scale * loudness
    return jnp.minimum(jnp.maximum(values, -bound), bound).astype(kind)


def setup_inputs(seed: int = 0, part: int = 0) -> dict:
    splits = jax.random.split(jax.random.key(seed), 10)
    own_keys = jax.random.split(jax.random.fold_in(splits[9], part), 10)
    return {
        "stream_in": bell_draw(own_keys[0], (ROWS, D), 0.1, 0.59765625, ((0, 4), (1, 4))),
        "attention_gain": jnp.clip(1.0 + 0.18 * jax.random.normal(splits[1], (D,), jnp.float32), 0.1, 1.9),
        "dense_gain": jnp.clip(1.0 + 0.18 * jax.random.normal(splits[2], (D,), jnp.float32), 0.1, 1.9),
        "w_query": bell_draw(splits[3], (D, QW), D ** -0.5, 0.0625, ((0, 4), (1, 4))),
        "w_keyval": bell_draw(splits[4], (D, 2 * KVW), D ** -0.5, 0.0625, ((0, 4),)),
        "w_out": bell_draw(splits[5], (QW, D), QW ** -0.5, 0.0625, ((0, 4), (1, 4))),
        "gate_up": bell_draw(splits[6], (D, 2, FF), D ** -0.5, 0.0625, ((0, 4), (2, 4))),
        "cache_entries": draw_cache_entries(jax.random.fold_in(jax.random.fold_in(splits[9], part), 71), part),
        "lengths": draw_lengths(jax.random.fold_in(jax.random.fold_in(splits[9], part), 71), part),
    }


rope_base = 500000.0
epsilon = 1e-05

def rotate(vectors, positions):
    half_dim = HD // 2
    frequency = jnp.exp(jnp.arange(half_dim, dtype=jnp.float32) * (-2.0 * math.log(rope_base) / HD))
    angles = positions.astype(jnp.float32)[:, None] * frequency[None, :]
    cosine = jnp.cos(angles)[:, None, :]
    sinus = jnp.sin(angles)[:, None, :]
    leading = vectors[..., :half_dim]
    trailing = vectors[..., half_dim:]
    return jnp.concatenate([leading * cosine - trailing * sinus, trailing * cosine + leading * sinus], axis=-1)

def attend(query_rot, key_rot, value_new, cache_entries, lengths):
    row_total = query_rot.shape[0]
    group_size = QH // KVH
    grouped = query_rot.astype(jnp.float32).reshape(row_total, KVH, group_size, HD)
    cached_keys = cache_entries[:, 0].astype(jnp.float32).reshape(row_total, CACHE, KVH, HD)
    cached_values = cache_entries[:, 1].astype(jnp.float32).reshape(row_total, CACHE, KVH, HD)
    score_scale = 1.0 / math.sqrt(HD)
    scores = jnp.einsum('rkgd,rtkd->rkgt', grouped, cached_keys) * score_scale
    own_score = jnp.einsum('rkgd,rkd->rkg', grouped, key_rot.astype(jnp.float32)) * score_scale
    visible = (jnp.arange(CACHE, dtype=jnp.int32)[None, :] < lengths[:, None])[:, None, None, :]
    highest = jnp.maximum(lax.optimization_barrier(jnp.max(jnp.where(visible, scores, -jnp.inf), axis=3)), own_score)
    expo_terms = jnp.where(visible, jnp.exp(scores - highest[..., None]), 0.0)
    own_weight = jnp.exp(own_score - highest)
    denominator = lax.optimization_barrier(jnp.sum(expo_terms, axis=3)) + own_weight
    rounded_w = expo_terms.astype(jnp.bfloat16).astype(jnp.float32)
    own_rounded = own_weight.astype(jnp.bfloat16).astype(jnp.float32)
    summed = jnp.einsum('rkgt,rtkd->rkgd', rounded_w, cached_values)
    summed = summed + own_rounded[..., None] * value_new.astype(jnp.float32)[:, :, None, :]
    return (summed / denominator[..., None]).astype(jnp.bfloat16).reshape(row_total, QW)

def reference(stream_in, attention_gain, dense_gain, w_query, w_keyval, w_out, gate_up, cache_entries, lengths):
    row_total = stream_in.shape[0]
    stream_f = stream_in.astype(jnp.float32)
    scale_one = lax.rsqrt(lax.optimization_barrier(jnp.mean(stream_f * stream_f, axis=1, keepdims=True)) + epsilon)
    normed = (stream_f * scale_one * attention_gain[None, :]).astype(jnp.bfloat16)
    queries = jnp.dot(normed, w_query, preferred_element_type=jnp.float32).astype(jnp.bfloat16)
    keyval = jnp.dot(normed, w_keyval, preferred_element_type=jnp.float32).astype(jnp.bfloat16)
    queries = lax.optimization_barrier(queries)
    keyval = lax.optimization_barrier(keyval)
    query_rot = rotate(queries.astype(jnp.float32).reshape(row_total, QH, HD), lengths).astype(jnp.bfloat16)
    key_rot = rotate(keyval[:, :KVW].astype(jnp.float32).reshape(row_total, KVH, HD), lengths).astype(jnp.bfloat16)
    value_new = keyval[:, KVW:]
    new_entries = jnp.concatenate([key_rot.reshape(row_total, KVW), value_new], axis=1)
    block_rows = ROWS_DEV
    block_count = row_total // block_rows

    def one_block(items):
        return attend(items[0], items[1], items[2], items[3], items[4])
    context = lax.map(one_block, (query_rot.reshape(block_count, block_rows, QH, HD), key_rot.reshape(block_count, block_rows, KVH, HD), value_new.reshape(block_count, block_rows, KVH, HD), cache_entries.reshape(block_count, block_rows, 2, CACHE, KVW), lengths.reshape(block_count, block_rows)))
    context = context.reshape(row_total, QW)
    residual = stream_f + jnp.dot(context, w_out, preferred_element_type=jnp.float32)
    stream = residual.astype(jnp.bfloat16)
    scale_two = lax.rsqrt(lax.optimization_barrier(jnp.mean(residual * residual, axis=1, keepdims=True)) + epsilon)
    normed_two = (residual * scale_two * dense_gain[None, :]).astype(jnp.bfloat16)
    shard_width = D // N_GX
    input_blocks = jnp.transpose(normed_two.reshape(row_total, N_GX, shard_width), (1, 0, 2))
    weight_blocks = gate_up.reshape(N_GX, shard_width, 2 * FF)

    def add_block(total, items):
        partial_value = jnp.dot(items[0], items[1], preferred_element_type=jnp.float32).astype(jnp.bfloat16)
        partial_value = lax.optimization_barrier(partial_value)
        return (total + partial_value.astype(jnp.float32), None)
    projected, _ = lax.scan(add_block, jnp.zeros((row_total, 2 * FF), jnp.float32), (input_blocks, weight_blocks))
    mlp_hidden = (jax.nn.silu(projected[:, :FF]) * projected[:, FF:]).astype(jnp.bfloat16)
    return (stream, mlp_hidden, new_entries)
```

```python
import functools
import math

import jax
import jax.numpy as jnp
from jax import lax
from jax.experimental import pallas as pl
from jax.experimental.pallas import tpu as pltpu
from jax.sharding import PartitionSpec as P

D = 8192
HD = 128
QH = 64
KVH = 4
CACHE = 384


rope_base = 500000.0
epsilon = 1e-05

VMEM_BYTES = 58 * 1024 * 1024
LANES = 128
f32 = jnp.float32
bf16 = jnp.bfloat16


def call(kernel, name, flops, moved, **kwargs):
    return pl.pallas_call(
        kernel,
        name=name,
        compiler_params=pltpu.CompilerParams(vmem_limit_bytes=VMEM_BYTES),
        cost_estimate=pl.CostEstimate(flops=flops, bytes_accessed=moved, transcendentals=0),
        **kwargs,
    )


def side_tile(sums):
    lane = lax.broadcasted_iota(jnp.int32, (sums.shape[0], LANES), 1)
    first = sums.astype(bf16).astype(f32)
    second = (sums - first).astype(bf16).astype(f32)
    third = sums - first - second
    tile = jnp.where(lane == 0, first, jnp.where(lane == 1, second, third))
    return jnp.where(lane < 3, tile, 0.0).astype(bf16)


def qkv_kernel(which, rows, gain, w_query, w_keyval, parcel, left, *, steps, cut):
    step = pl.program_id(0)
    count = rows.shape[0]
    device_rows = parcel.shape[1]
    query_cols = steps * cut
    keyval_cols = w_keyval.shape[1]

    def put(values, start, size):
        for place in range(parcel.shape[0]):
            parcel[place, :, pl.ds(start, size)] = values[
                place * device_rows : (place + 1) * device_rows
            ].astype(bf16)

    def product(weights):
        both = jnp.dot(left[...], weights, preferred_element_type=f32)
        return both[:count] + both[count:]

    @pl.when(step == 0)
    def _():
        wide = rows[...].astype(f32)
        gained = wide * gain[...]
        coarse = gained.astype(bf16)
        left[:count] = coarse
        left[count:] = (gained - coarse.astype(f32)).astype(bf16)
        squares = jnp.sum(wide * wide, axis=1, keepdims=True)
        put(side_tile(squares).astype(f32), query_cols + keyval_cols, LANES)
        put(product(w_keyval[...]), query_cols, keyval_cols)

    put(product(w_query[...]), pl.multiple_of(step * cut, LANES), cut)


def project_qkv(rows, gain, w_query, w_keyval, gy_count, places, device_rows):
    count, width = rows.shape
    query_cols = w_query.shape[1]
    keyval_cols = w_keyval.shape[1] // gy_count
    cut = min(512, query_cols)
    steps = query_cols // cut
    parcel_cols = query_cols + keyval_cols + LANES
    index = lax.axis_index("gy").astype(jnp.int32).reshape(1)
    return call(
        functools.partial(qkv_kernel, steps=steps, cut=cut),
        "qkv",
        4 * count * width * (query_cols + keyval_cols),
        2 * width * (query_cols + keyval_cols),
        grid_spec=pltpu.PrefetchScalarGridSpec(
            num_scalar_prefetch=1,
            grid=(steps,),
            in_specs=[
                pl.BlockSpec((count, width), lambda n, s: (0, 0)),
                pl.BlockSpec((1, width), lambda n, s: (0, 0)),
                pl.BlockSpec((width, cut), lambda n, s: (0, n)),
                pl.BlockSpec((width, keyval_cols), lambda n, s: (0, s[0])),
            ],
            out_specs=pl.BlockSpec((places, device_rows, parcel_cols), lambda n, s: (0, 0, 0)),
            scratch_shapes=[pltpu.VMEM((2 * count, width), bf16)],
        ),
        out_shape=jax.ShapeDtypeStruct((places, device_rows, parcel_cols), bf16),
    )(index, rows, gain.reshape(1, width), w_query, w_keyval)


def attend_kernel(
    arrived, cosine, sinus, lengths, cache, context, entries, *, gx_count, gy_count, query_cols
):
    head = pl.program_id(0)
    device_rows = arrived.shape[1]
    keyval_cols = 2 * KVH * HD // gy_count
    heads_in = query_cols // HD
    parcels = gy_count // KVH
    blocks_in = keyval_cols // HD
    group = parcels * heads_in
    total = group * device_rows

    def summed(parcel, start, size):
        values = arrived[parcel, :, pl.ds(start, size)].astype(f32)
        for block in range(1, gx_count):
            values = values + arrived[block * gy_count + parcel, :, pl.ds(start, size)].astype(f32)
        return values

    squares = jnp.sum(summed(0, query_cols + keyval_cols, LANES), axis=1, keepdims=True)
    scale = lax.rsqrt(squares / D + epsilon)

    def taken(parcel, start, size):
        return (summed(parcel, start, size) * scale).astype(bf16).astype(f32)

    def turned(values, cosines, sines):
        return values * cosines + pltpu.roll(values, HD // 2, 1) * sines

    def keyval_block(number):
        start = query_cols + (number % blocks_in) * HD
        return taken(number // blocks_in, pl.multiple_of(start, LANES), HD)

    def spread(values):
        return jnp.concatenate([values] * group, axis=0)

    pieces = []
    for parcel in range(parcels):
        values = taken(head * parcels + parcel, 0, query_cols)
        pieces += [values[:, n * HD : (n + 1) * HD] for n in range(heads_in)]
    query_rot = turned(jnp.concatenate(pieces, axis=0), cosine[...], sinus[...]).astype(bf16)
    key_rot = turned(keyval_block(head), cosine[:device_rows], sinus[:device_rows]).astype(bf16)
    value_new = keyval_block(KVH + head)
    entries[:, pl.ds(pl.multiple_of(head * HD, LANES), HD)] = key_rot
    entries[:, pl.ds(pl.multiple_of((KVH + head) * HD, LANES), HD)] = value_new.astype(bf16)

    score_scale = 1.0 / math.sqrt(HD)
    own = jnp.sum(query_rot.astype(f32) * spread(key_rot.astype(f32)), axis=1, keepdims=True)
    own = own * score_scale
    row_of = lax.broadcasted_iota(jnp.int32, (total, CACHE), 0) % device_rows
    slot = lax.broadcasted_iota(jnp.int32, (total, CACHE), 1)
    scores = jnp.zeros((total, CACHE), f32)
    for row in range(device_rows):
        found = lax.dot_general(
            query_rot, cache[row, 0], (((1,), (1,)), ((), ())), preferred_element_type=f32
        )
        scores = jnp.where(row_of == row, found, scores)
    scores = jnp.where(slot < lengths[...], scores * score_scale, -jnp.inf)
    top = jnp.maximum(jnp.max(scores, axis=1, keepdims=True), own)
    terms = jnp.exp(scores - top)
    own_weight = jnp.exp(own - top)
    denominator = jnp.sum(terms, axis=1, keepdims=True) + own_weight
    gathered = own_weight.astype(bf16).astype(f32) * spread(value_new)
    for row in range(device_rows):
        weights = jnp.where(row_of == row, terms, 0.0).astype(bf16)
        gathered = gathered + jnp.dot(weights, cache[row, 1], preferred_element_type=f32)
    result = gathered / denominator
    for parcel in range(parcels):
        for n in range(heads_in):
            first = (parcel * heads_in + n) * device_rows
            context[parcel, :, n * HD : (n + 1) * HD] = result[first : first + device_rows].astype(
                bf16
            )


def attend(arrived, cache_entries, lengths, gx_count, gy_count, query_cols):
    device_rows = lengths.shape[0]
    group = QH // KVH
    half_dim = HD // 2
    frequency = jnp.exp(jnp.arange(half_dim, dtype=f32) * (-2.0 * math.log(rope_base) / HD))
    angles = lengths.astype(f32)[:, None] * frequency[None, :]
    cosine = jnp.cos(angles)
    sinus = jnp.sin(angles)
    cosine = jnp.tile(jnp.concatenate([cosine, cosine], axis=1), (group, 1))
    sinus = jnp.tile(jnp.concatenate([-sinus, sinus], axis=1), (group, 1))
    limits = jnp.tile(lengths.reshape(device_rows, 1), (group, 1))
    total = group * device_rows
    parcels = gy_count // KVH
    return call(
        functools.partial(
            attend_kernel, gx_count=gx_count, gy_count=gy_count, query_cols=query_cols
        ),
        "attend",
        4 * total * HD * CACHE * KVH * device_rows,
        2 * cache_entries.size,
        grid=(KVH,),
        in_specs=[
            pl.BlockSpec(arrived.shape, lambda k: (0, 0, 0)),
            pl.BlockSpec((total, HD), lambda k: (0, 0)),
            pl.BlockSpec((total, HD), lambda k: (0, 0)),
            pl.BlockSpec((total, 1), lambda k: (0, 0)),
            pl.BlockSpec((device_rows, 2, CACHE, HD), lambda k: (0, 0, 0, k)),
        ],
        out_specs=[
            pl.BlockSpec((parcels, device_rows, query_cols), lambda k: (k, 0, 0)),
            pl.BlockSpec((device_rows, 2 * KVH * HD), lambda k: (0, 0)),
        ],
        out_shape=[
            jax.ShapeDtypeStruct((gy_count, device_rows, query_cols), bf16),
            jax.ShapeDtypeStruct((device_rows, 2 * KVH * HD), bf16),
        ],
    )(arrived, cosine, sinus, limits, cache_entries)


def out_kernel(rows, weights, result):
    result[...] = jnp.dot(rows[...], weights[...], preferred_element_type=f32)


def project_out(rows, weights):
    count, width = rows.shape
    cols = weights.shape[1]
    cut = min(512, cols)
    return call(
        out_kernel,
        "out",
        2 * count * width * cols,
        2 * width * cols,
        grid=(cols // cut,),
        in_specs=[
            pl.BlockSpec((count, width), lambda n: (0, 0)),
            pl.BlockSpec((width, cut), lambda n: (0, n)),
        ],
        out_specs=pl.BlockSpec((count, cut), lambda n: (0, n)),
        out_shape=jax.ShapeDtypeStruct((count, cols), f32),
    )(rows, weights)


def sum_and_spread(partial_out, stream_in, rows_in, dense_gain):
    gy_count = lax.axis_size("gy")
    gy_index = lax.axis_index("gy")
    width = partial_out.shape[1]

    def gained_rows(residual):
        squares = jnp.sum(residual * residual, axis=1, keepdims=True)
        gained = (residual * dense_gain[None, :]).astype(bf16)
        return jnp.concatenate([gained, side_tile(squares)], axis=1)

    if gy_count != 4:
        blocks = partial_out.astype(bf16).reshape(gy_count, -1, width)
        blocks = lax.all_to_all(blocks, "gy", split_axis=0, concat_axis=0, tiled=True)
        residual = stream_in.astype(f32) + jnp.sum(blocks.astype(f32), axis=0)
        gathered = lax.all_gather(gained_rows(residual), "gy", axis=0, tiled=True)
        return residual.astype(bf16), gathered

    core = gy_index % 2
    chip = gy_index // 2
    core_pairs = [(0, 1), (1, 0), (2, 3), (3, 2)]
    chip_pairs = [(0, 2), (2, 0), (1, 3), (3, 1)]

    def halves(values):
        blocks = values.reshape(2, 2, -1, width)
        first = blocks[:, 0].reshape(-1, width)
        second = blocks[:, 1].reshape(-1, width)
        return first, second

    first, second = halves(partial_out)
    sent = jnp.where(core == 0, second, first).astype(bf16)
    pair_sum = jnp.where(core == 0, first, second) + lax.ppermute(sent, "gy", core_pairs).astype(f32)
    other = lax.ppermute(pair_sum.astype(bf16), "gy", chip_pairs).astype(f32)
    first, second = halves(rows_in)
    residual = jnp.where(core == 0, first, second).astype(f32) + (pair_sum + other)
    count = stream_in.shape[0]
    stream = jnp.where(chip == 0, residual[:count], residual[count:]).astype(bf16)
    mine = gained_rows(residual)
    theirs = lax.ppermute(mine, "gy", core_pairs)
    even = jnp.where(core == 0, mine, theirs)
    odd = jnp.where(core == 0, theirs, mine)
    gathered = jnp.concatenate([even[:count], odd[:count], even[count:], odd[count:]], axis=0)
    return stream, gathered


def mlp_kernel(rows, weights, *rest, steps, side):
    results, total = rest[:-1], rest[-1]
    step = pl.program_id(0)
    depth, tiles = weights.shape[0], weights.shape[1]
    block = weights[...].reshape(depth, tiles * 2 * LANES)
    product = jnp.dot(rows[:, :depth], block, preferred_element_type=f32)

    @pl.when(step == 0)
    def _():
        total[...] = product

    @pl.when(step > 0)
    def _():
        total[...] += product

    @pl.when(step == steps - 1)
    def _():
        size = results[0].shape[0]
        for place, result in enumerate(results):
            result[:, : tiles * 2 * LANES] = total[place * size : (place + 1) * size].astype(bf16)


def gate_up_part(rows, view, part, tiles, places):
    count = rows.shape[0]
    width = view.shape[0]
    cols = tiles * 2 * LANES
    depth = min(512, width)
    steps = width // depth
    return call(
        functools.partial(mlp_kernel, steps=steps, side=0),
        "gate_up_%d" % part,
        2 * count * width * cols,
        2 * width * cols,
        grid=(steps,),
        in_specs=[
            pl.BlockSpec((count, depth), lambda k: (0, k)),
            pl.BlockSpec((depth, tiles, 2, LANES), lambda k: (k, part, 0, 0)),
        ],
        out_specs=[pl.BlockSpec((count // places, cols), lambda k: (0, 0))] * places,
        out_shape=[jax.ShapeDtypeStruct((count // places, cols), bf16)] * places,
        scratch_shapes=[pltpu.VMEM((count, cols), f32)],
    )(rows, view)


def hidden_kernel(sides, *refs, parts, places):
    result = refs[-1]
    squares = jnp.zeros((sides.shape[1], 1), f32)
    for place in range(places):
        squares = squares + jnp.sum(sides[place].astype(f32), axis=1, keepdims=True)
    scale = lax.rsqrt(squares / D + epsilon)
    start = 0
    for part in range(parts):
        blocks = refs[part * places : (part + 1) * places]
        tiles = blocks[0].shape[1] // (2 * LANES)
        for tile in range(tiles):
            def added(first):
                values = blocks[0][:, first : first + LANES].astype(f32)
                for block in blocks[1:]:
                    values = values + block[:, first : first + LANES].astype(f32)
                return values * scale

            gate = added(tile * 2 * LANES)
            up = added(tile * 2 * LANES + LANES)
            hidden = gate / (1.0 + jnp.exp(-gate)) * up
            result[:, start : start + LANES] = hidden.astype(bf16)
            start += LANES


def exchange(blocks):
    count = len(blocks)
    arrived = [blocks[0]]
    for shift in range(1, count):
        pairs = [(n, (n + shift) % count) for n in range(count)]
        arrived.append(lax.ppermute(blocks[shift], "gx", pairs))
    return arrived


def on_device(
    stream_in, attention_gain, dense_gain, w_query, w_keyval, w_out, gate_up, cache_entries, lengths
):
    gx_count = lax.axis_size("gx")
    gy_count = lax.axis_size("gy")
    gx_index = lax.axis_index("gx")
    width = stream_in.shape[1]
    device_rows = lengths.shape[0]
    query_cols = w_query.shape[1]
    hidden_cols = gate_up.shape[2]
    places = gx_count * gy_count

    rows_in = lax.all_gather(stream_in, "gy", axis=0, tiled=True)
    parcel = project_qkv(
        rows_in, attention_gain, w_query, w_keyval, gy_count, places, device_rows
    )
    arrived = lax.all_to_all(parcel, ("gx", "gy"), split_axis=0, concat_axis=0, tiled=True)
    context, new_entries = attend(
        arrived, cache_entries, lengths, gx_count, gy_count, query_cols
    )
    blocks = jnp.broadcast_to(context[None], (gx_count,) + context.shape)
    blocks = blocks.reshape((places,) + context.shape[1:])
    head_rows = lax.all_to_all(blocks, ("gx", "gy"), split_axis=0, concat_axis=0, tiled=True)
    partial_out = project_out(head_rows.reshape(places * device_rows, query_cols), w_out)
    stream, gathered = sum_and_spread(partial_out, stream_in, rows_in, dense_gain)

    count = gathered.shape[0]
    size = count // gx_count
    turned = lax.dynamic_slice_in_dim(
        jnp.concatenate([gathered, gathered], axis=0), gx_index * size, count, 0
    )
    tiles = hidden_cols // LANES
    view = jnp.swapaxes(gate_up.reshape(width, 2, tiles, LANES), 1, 2)
    cut = 13 if tiles % 13 == 0 else 1
    parts = tiles // cut
    sides = exchange([turned[n * size : (n + 1) * size, width:] for n in range(gx_count)])
    received = []
    for part in range(parts):
        made = gate_up_part(turned, view, part, cut, gx_count)
        received += exchange(made)
    mlp_hidden = call(
        functools.partial(hidden_kernel, parts=parts, places=gx_count),
        "hidden",
        8 * size * hidden_cols * gx_count,
        4 * size * hidden_cols * gx_count,
        out_shape=jax.ShapeDtypeStruct((size, hidden_cols), bf16),
    )(jnp.stack(sides, axis=0), *received)
    return (stream, mlp_hidden, new_entries)


def solution(mesh):
    placed = (
        P(("grp", "gy"), "gx"),
        P("gx"),
        P("gx"),
        P("gx", "gy"),
        P("gx", None),
        P("gy", "gx"),
        P("gx", None, "gy"),
        P(("grp", "gx", "gy"), None, None, None),
        P(("grp", "gx", "gy")),
    )
    return jax.shard_map(
        on_device,
        mesh=mesh,
        in_specs=placed,
        out_specs=(P(("grp", "gy"), "gx"), P(("grp", "gx"), "gy"), P(("grp", "gx", "gy"), None)),
        check_vma=False,
    )
```
